256 devices in a mesh: dp: 16 (over y, x), shard: 16 (over z, core).
Axes of the slice: x: 4, y: 4, z: 8, core: 2. Of those that a mesh axis runs over, the one named last changes fastest.
Arguments:
- grad_parts: bfloat16 [16, 16, 1536, 1536], P('dp', None, 'shard'), may hold values from -48 to 48
- momentum_owned: float32 [16, 16, 96, 1536], P('shard', None, 'dp'), may hold values from -6 to 6
- owner_table: int32 [16], replicated, may hold values from 0 to 15, each once
- step_offset: int32 [1], replicated, may hold values from 0 to 15
Outputs:
- updates: bfloat16 [16, 1536, 1536], P('dp', 'shard')
- new_momentum: float32 [16, 16, 96, 1536], P('shard', None, 'dp')
The draws below stay inside these ranges and needn't reach their ends.
Inputs may be any that keep to these rules, and one draw needn't show every extreme that they name: `owner_table`: each owner slot is named by exactly one matrix.
All inputs are finite; a program needn't handle non-finite values.
Results may differ from the reference program's by a relative error of at most 0.0089.
Values may be sent and summed in bfloat16 or wider, within the bound.
No kernel may reach another device: no remote copies, remote signals or barrier semaphores. Data moves between devices by JAX's collectives and lax.ppermute only.
A program may use at most 64 MiB of HBM per device.

```python
import math
import jax
import jax.numpy as jnp
from jax import lax

D = 1536
ITERS = 2
MATS = 16
PIECE = 96
N_DP = 16
N_SHARD = 16


def draw_grad_parts(key, part):
    key = jax.random.fold_in(key, 11)
    key_left, key_right, key_noise, key_rows = jax.random.split(key, 4)
    left = jax.random.truncated_normal(key_left, -3.0, 3.0, (MATS, D, 4), jnp.float32)
    right = jax.random.truncated_normal(key_right, -3.0, 3.0, (MATS, 4, D), jnp.float32)
    lowrank = 0.5 * (left[:, :, 0:1] * right[:, 0:1, :] + left[:, :, 1:2] * right[:, 1:2, :] + left[:, :, 2:3] * right[:, 2:3, :] + left[:, :, 3:4] * right[:, 3:4, :])
    noise = jax.random.truncated_normal(key_noise, -3.0, 3.0, (N_DP, MATS, D, D), jnp.float32)
    rise = 3.0
    rows = jnp.arange(D, dtype=jnp.int32)
    piece_rows = D // N_SHARD
    sub_rows = piece_rows // N_DP
    level = (rows % piece_rows // sub_rows).astype(jnp.float32) / max(N_DP - 1, 1)
    base_scale = jnp.exp(jax.random.uniform(key_rows, (MATS, D), jnp.float32, math.log(0.5), math.log(2.0)))
    row_scale = base_scale * jnp.power(rise, level - 0.5)[None, :]
    values = row_scale[None, :, :, None] * (lowrank[None] / N_DP + 0.6 * noise / math.sqrt(N_DP))
    return values.astype(jnp.bfloat16)


def block_scale(stream_key, extent, shards, low, top_value):
    level = 1.0
    for dim, blocks in shards:
        draws = jax.random.uniform(jax.random.fold_in(jax.random.fold_in(stream_key, 6), dim), (blocks,), jnp.float32, low / len(shards), top_value / len(shards))
        level = level * jnp.repeat(jnp.exp(draws), extent[dim] // blocks).reshape((-1,) + (1,) * (len(extent) - 1 - dim))
    return level


def normal_values(own_key, shape, deviation, reach, pieces=(), kind=jnp.bfloat16):
    result = jax.random.normal(own_key, shape, jnp.float32) * deviation
    if len(pieces) > 0:
        result = block_scale(own_key, shape, pieces, -0.22, 0.18) * result
    return jnp.clip(result, min=-reach, max=reach).astype(kind)


def setup_inputs(seed: int = 0) -> dict:
    splits = jax.random.split(jax.random.key(seed), 5)
    return {
        "grad_parts": draw_grad_parts(jax.random.fold_in(splits[4], 71), 0),
        "momentum_owned": normal_values(splits[1], (N_SHARD, N_SHARD, PIECE, D), 1.0, 6.0, ((0, 16), (2, 16)), jnp.float32),
        "owner_table": jax.random.permutation(splits[2], N_SHARD).astype(jnp.int32),
        "step_offset": jax.random.randint(splits[3], (1,), 0, N_SHARD).astype(jnp.int32),
    }


momentum_decay = 0.95
linear_coef = 3.4445
cubic_coef = -4.775
quintic_coef = 2.0315

def transpose_dot(left, right):
    return lax.dot_general(left, right, (((1,), (1,)), ((), ())), preferred_element_type=jnp.float32)

def reference(grad_parts, momentum_owned, owner_table, step_offset):
    owner_slot = ((owner_table + step_offset[0]) % N_SHARD).astype(jnp.int32)

    def single(matrix_index):
        parts = lax.dynamic_index_in_dim(grad_parts, matrix_index, 1, keepdims=False)
        grad = lax.optimization_barrier(jnp.sum(parts.astype(jnp.float32), axis=0)).astype(jnp.bfloat16)
        slot = owner_slot[matrix_index]
        previous = lax.dynamic_index_in_dim(momentum_owned, slot, 0, keepdims=False).reshape(D, D)
        moment = momentum_decay * previous + grad.astype(jnp.float32)
        nesterov = grad.astype(jnp.float32) + momentum_decay * moment
        iterate = (nesterov / (jnp.sqrt(jnp.sum(nesterov * nesterov)) + 1e-07)).astype(jnp.bfloat16)
        mixed = iterate.astype(jnp.float32)
        for sweep in range(ITERS):
            gram = transpose_dot(iterate, iterate).astype(jnp.bfloat16)
            first = jnp.dot(gram, iterate, preferred_element_type=jnp.float32)
            first_low = first.astype(jnp.bfloat16)
            second = jnp.dot(gram, first_low, preferred_element_type=jnp.float32)
            mixed = linear_coef * iterate.astype(jnp.float32) + cubic_coef * first + quintic_coef * second
            if sweep + 1 < ITERS:
                iterate = mixed.astype(jnp.bfloat16)
        update = (mixed * lax.rsqrt(jnp.mean(mixed * mixed) + 1e-06)).astype(jnp.bfloat16)
        return (update, moment)
    updates, moments = lax.map(single, jnp.arange(MATS, dtype=jnp.int32))
    owner_order = jnp.argsort(owner_slot).astype(jnp.int32)
    new_momentum = jnp.take(moments, owner_order, axis=0).reshape(N_SHARD, N_SHARD, D // N_SHARD, D)
    return (updates, new_momentum)
```

```python
import jax
import jax.numpy as jnp
from jax import lax
from jax.experimental import pallas as pl
from jax.experimental.pallas import tpu as pltpu
from jax.sharding import PartitionSpec as P

D = 1536
ITERS = 2
CHUNKS = 2
TILE = 512

momentum_decay = 0.95
linear_coef = 3.4445
cubic_coef = -4.775
quintic_coef = 2.0315


def swap(value, axis):
    return lax.all_to_all(value, axis, split_axis=0, concat_axis=0, tiled=True)


def xor_swap(value, axis):
    count = value.shape[0]
    step = 1
    while step < count:
        pairs = [(i, i ^ step) for i in range(count)]
        halves = value.reshape((count // (2 * step), 2, step) + value.shape[1:])
        other = lax.ppermute(halves[:, 1], axis, pairs)
        value = jnp.stack([halves[:, 0], other], axis=1).reshape(value.shape)
        step *= 2
    return value


def upper_tile(t):
    i = (t >= 3).astype(jnp.int32) + (t >= 5).astype(jnp.int32)
    return i, t - 2 * i + (i * (i - 1)) // 2


def newton_schulz_kernel(shard_ref, *refs):
    parts = refs[:CHUNKS]
    out_ref, gram_ref, poly_ref, mixed_ref, diag_ref, square_ref = refs[CHUNKS : CHUNKS + 6]
    later = refs[CHUNKS + 6 :]
    wide = D // CHUNKS
    tiles = D // TILE
    contract_last = (((1,), (1,)), ((), ()))

    def block(t):
        return pl.ds(pl.multiple_of(t * TILE, TILE), TILE)

    def sweep(sources, store, measured):
        diag_ref[...] = jnp.zeros_like(diag_ref)

        def gram_tile(t, carry):
            i, j = upper_tile(t)
            total = jnp.zeros((TILE, TILE), jnp.float32)
            for source in sources:
                total = total + lax.dot_general(
                    source[block(i), :], source[block(j), :], contract_last, preferred_element_type=jnp.float32
                )
            low = total.astype(jnp.bfloat16)
            gram_ref[block(i), block(j)] = low

            @pl.when(i != j)
            def _():
                gram_ref[block(j), block(i)] = low.T

            if measured:

                @pl.when(i == j)
                def _():
                    rows = lax.broadcasted_iota(jnp.int32, (TILE, TILE), 0)
                    columns = lax.broadcasted_iota(jnp.int32, (TILE, TILE), 1)
                    diag_ref[...] += jnp.sum(jnp.where(rows == columns, total, 0.0), axis=0, keepdims=True)

            return carry

        lax.fori_loop(0, tiles * (tiles + 1) // 2, gram_tile, 0)
        if measured:
            inverse = 1.0 / (jnp.sqrt(jnp.sum(diag_ref[...])) + 1e-07)
            cubic = cubic_coef * (inverse * inverse)
            quintic = quintic_coef * (inverse * inverse) * (inverse * inverse)
        else:
            inverse, cubic, quintic = 1.0, cubic_coef, quintic_coef

        def poly_tile(t, carry):
            i, j = upper_tile(t)
            total = jnp.dot(gram_ref[block(i), :], gram_ref[:, block(j)], preferred_element_type=jnp.float32)
            low = (cubic * gram_ref[block(i), block(j)].astype(jnp.float32) + quintic * total).astype(jnp.bfloat16)
            poly_ref[block(i), block(j)] = low

            @pl.when(i != j)
            def _():
                poly_ref[block(j), block(i)] = low.T

            return carry

        lax.fori_loop(0, tiles * (tiles + 1) // 2, poly_tile, 0)

        def mix_tile(i, carry):
            for c, source in enumerate(sources):
                total = jnp.dot(poly_ref[block(i), :], source[...], preferred_element_type=jnp.float32)
                store(i, c, (linear_coef * source[block(i), :].astype(jnp.float32) + total) * inverse)
            return carry

        lax.fori_loop(0, tiles, mix_tile, 0)

    def store_later(i, c, mixed):
        later[c][block(i), :] = mixed.astype(jnp.bfloat16)

    def store_mixed(i, c, mixed):
        mixed_ref[block(i), c * wide : (c + 1) * wide] = mixed
        square_ref[...] += jnp.sum(mixed * mixed, axis=0, keepdims=True)

    square_ref[...] = jnp.zeros_like(square_ref)
    sweep(parts, store_later, True)
    sweep(later, store_mixed, False)
    scale = lax.rsqrt(jnp.sum(square_ref[...]) / (D * D) + 1e-06)
    rows = out_ref.shape[0]
    mine = pl.ds(pl.multiple_of(shard_ref[0] * rows, rows), rows)
    out_ref[...] = (mixed_ref[mine, :] * scale).astype(jnp.bfloat16)


def newton_schulz(parts, shard_index, rows):
    wide = D // CHUNKS
    return pl.pallas_call(
        newton_schulz_kernel,
        out_shape=jax.ShapeDtypeStruct((rows, D), jnp.bfloat16),
        in_specs=[pl.BlockSpec(memory_space=pltpu.SMEM)]
        + [pl.BlockSpec(memory_space=pltpu.VMEM)] * CHUNKS,
        out_specs=pl.BlockSpec(memory_space=pltpu.VMEM),
        scratch_shapes=[
            pltpu.VMEM((D, D), jnp.bfloat16),
            pltpu.VMEM((D, D), jnp.bfloat16),
            pltpu.VMEM((D, D), jnp.float32),
            pltpu.VMEM((1, TILE), jnp.float32),
            pltpu.VMEM((1, wide), jnp.float32),
        ]
        + [pltpu.VMEM((D, wide), jnp.bfloat16)] * CHUNKS,
        compiler_params=pltpu.CompilerParams(vmem_limit_bytes=44 * 1024 * 1024),
        cost_estimate=pl.CostEstimate(
            flops=2 * ITERS * 7 * D * D * D // 3, bytes_accessed=D * D * 2, transcendentals=0
        ),
        name="newton_schulz",
    )(shard_index, *parts)


def body(grad_parts, momentum_owned, owner_table, step_offset):
    shard_count = lax.axis_size("shard")
    replica, shard = lax.axis_index("dp"), lax.axis_index("shard")
    piece_rows = grad_parts.shape[2]
    sub_rows = momentum_owned.shape[2]
    owner_slot = (owner_table + step_offset[0]) % shard_count
    slot_ids = jnp.arange(shard_count, dtype=jnp.int32)
    owner_order = jnp.sum(
        jnp.where(owner_slot[None, :] == slot_ids[:, None], slot_ids[None, :], 0), axis=1
    )
    momentum = momentum_owned[0]

    by_slot = xor_swap(jnp.take(momentum.astype(jnp.bfloat16), slot_ids ^ shard, axis=0), "shard")
    by_matrix = jnp.take(by_slot, jnp.take(owner_slot, slot_ids ^ replica) ^ shard, axis=0)
    own_momentum = jnp.take(xor_swap(by_matrix, "dp"), slot_ids ^ replica, axis=0).reshape(piece_rows, D)

    wide = D // CHUNKS
    grads, gathered = [], []
    for c in range(CHUNKS):
        columns = slice(c * wide, (c + 1) * wide)
        parts = swap(grad_parts[0, :, :, columns], "dp")
        summed = lax.optimization_barrier(jnp.sum(parts.astype(jnp.float32), axis=0))
        grad = summed.astype(jnp.bfloat16)
        grad_float = grad.astype(jnp.float32)
        moment_here = momentum_decay * own_momentum[:, columns].astype(jnp.float32) + grad_float
        nesterov = (grad_float + momentum_decay * moment_here).astype(jnp.bfloat16)
        grads.append(grad)
        gathered.append(lax.all_gather(nesterov, "shard", axis=0, tiled=True))

    grad = jnp.concatenate(grads, axis=1)
    by_matrix = swap(grad.reshape(-1, sub_rows, D), "dp")
    grad_rows = swap(jnp.take(by_matrix, owner_order, axis=0), "shard")
    moment = momentum_decay * momentum + grad_rows.astype(jnp.float32)

    update = newton_schulz(gathered, shard.astype(jnp.int32)[None], piece_rows)
    return (update[None], moment[None])


def solution(mesh):
    placed = (P("dp", None, "shard", None), P("shard", None, "dp", None), P(), P())
    return jax.shard_map(
        body,
        mesh=mesh,
        in_specs=placed,
        out_specs=(P("dp", "shard", None), P("shard", None, "dp", None)),
        check_vma=False,
    )
```

```python
import jax
import jax.numpy as jnp
from jax import lax
from jax.experimental import pallas as pl
from jax.experimental.pallas import tpu as pltpu
from jax.sharding import PartitionSpec as P

D = 1536
ITERS = 2
TILE = 512

momentum_decay = 0.95
linear_coef = 3.4445
cubic_coef = -4.775
quintic_coef = 2.0315


def swap(value, axis):
    return lax.all_to_all(value, axis, split_axis=0, concat_axis=0, tiled=True)


def xor_swap(value, axis):
    count = value.shape[0]
    step = 1
    while step < count:
        pairs = [(i, i ^ step) for i in range(count)]
        halves = value.reshape((count // (2 * step), 2, step) + value.shape[1:])
        other = lax.ppermute(halves[:, 1], axis, pairs)
        value = jnp.stack([halves[:, 0], other], axis=1).reshape(value.shape)
        step *= 2
    return value


def newton_schulz_kernel(place_ref, whole_ref, out_ref, first_ref, later_ref, gram_ref, poly_ref, mixed_ref, diag_ref, square_ref, sems):
    half = D // 2
    tiles = D // TILE
    contract_last = (((1,), (1,)), ((), ()))
    copies = [
        pltpu.make_async_copy(
            whole_ref.at[pl.ds(h * half, half), :], first_ref.at[pl.ds(h * half, half), :], sems.at[h]
        )
        for h in range(2)
    ]
    for copy in copies:
        copy.start()
    diag_ref[...] = jnp.zeros_like(diag_ref)
    square_ref[...] = jnp.zeros_like(square_ref)
    for copy in copies:
        copy.wait()

    def span(start, size):
        return pl.ds(pl.multiple_of(start, 256), size)

    def symmetric(product, finish, target):
        def step(t, carry):
            i = (t >= 2).astype(jnp.int32) * TILE
            j = (1 + (t >= 1).astype(jnp.int32)) * TILE
            k = t * TILE
            small = TILE // 2
            for row, column, height, diagonal in (
                (i, j, TILE, False),
                (i, j + small, TILE, False),
                (k, k, TILE, True),
                (k + small, k + small, small, True),
            ):
                low = finish(row, column, height, diagonal, product(row, column, height))
                target[span(row, height), span(column, small)] = low
                if not diagonal:
                    target[span(column, small), span(row, height)] = low.T
                elif height == TILE:
                    target[span(column, small), span(row + small, small)] = low[small:, :].T
            return carry

        lax.fori_loop(0, tiles, step, 0)

    def sweep(source, store, measured):
        def gram_product(row, column, height):
            return lax.dot_general(
                source[span(row, height), :],
                source[span(column, TILE // 2), :],
                contract_last,
                preferred_element_type=jnp.float32,
            )

        def gram_finish(row, column, height, diagonal, total):
            if measured and diagonal:
                rows = lax.broadcasted_iota(jnp.int32, total.shape, 0)
                columns = lax.broadcasted_iota(jnp.int32, total.shape, 1)
                diag_ref[...] += jnp.sum(jnp.where(rows == columns, total, 0.0), axis=0, keepdims=True)
            return total.astype(jnp.bfloat16)

        symmetric(gram_product, gram_finish, gram_ref)
        if measured:
            inverse = 1.0 / (jnp.sqrt(jnp.sum(diag_ref[...])) + 1e-07)
            cubic = cubic_coef * (inverse * inverse)
            quintic = quintic_coef * (inverse * inverse) * (inverse * inverse)
        else:
            inverse, cubic, quintic = 1.0, cubic_coef, quintic_coef

        def poly_product(row, column, height):
            return jnp.dot(
                gram_ref[span(row, height), :], gram_ref[:, span(column, TILE // 2)], preferred_element_type=jnp.float32
            )

        def poly_finish(row, column, height, diagonal, total):
            gram = gram_ref[span(row, height), span(column, TILE // 2)].astype(jnp.float32)
            return (cubic * gram + quintic * total).astype(jnp.bfloat16)

        symmetric(poly_product, poly_finish, poly_ref)

        def mix_tile(t, carry):
            rows = span(t * TILE, TILE)
            for c in range(0, D, TILE // 2):
                columns = slice(c, c + TILE // 2)
                total = jnp.dot(poly_ref[rows, :], source[:, columns], preferred_element_type=jnp.float32)
                store(rows, columns, (linear_coef * source[rows, columns].astype(jnp.float32) + total) * inverse)
            return carry

        lax.fori_loop(0, tiles, mix_tile, 0)

    def store_later(rows, columns, mixed):
        later_ref[rows, columns] = mixed.astype(jnp.bfloat16)

    def store_mixed(rows, columns, mixed):
        mixed_ref[rows, columns] = mixed
        square_ref[:, columns] += jnp.sum(mixed * mixed, axis=0, keepdims=True)

    sweep(first_ref, store_later, True)
    sweep(later_ref, store_mixed, False)
    scale = lax.rsqrt(jnp.sum(square_ref[...]) / (D * D) + 1e-06)
    rows = out_ref.shape[0]
    mine = pl.ds(pl.multiple_of(place_ref[0] * rows, rows), rows)
    out_ref[...] = (mixed_ref[mine, :] * scale).astype(jnp.bfloat16)


def newton_schulz(whole, place, rows):
    return pl.pallas_call(
        newton_schulz_kernel,
        out_shape=jax.ShapeDtypeStruct((rows, D), jnp.bfloat16),
        in_specs=[pl.BlockSpec(memory_space=pltpu.SMEM)] + [pl.BlockSpec(memory_space=pl.ANY)],
        out_specs=pl.BlockSpec(memory_space=pltpu.VMEM),
        scratch_shapes=[
            pltpu.VMEM((D, D), jnp.bfloat16),
            pltpu.VMEM((D, D), jnp.bfloat16),
            pltpu.VMEM((D, D), jnp.bfloat16),
            pltpu.VMEM((D, D), jnp.bfloat16),
            pltpu.VMEM((D, D), jnp.float32),
            pltpu.VMEM((1, TILE // 2), jnp.float32),
            pltpu.VMEM((1, D), jnp.float32),
            pltpu.SemaphoreType.DMA((2,)),
        ],
        compiler_params=pltpu.CompilerParams(vmem_limit_bytes=48 * 1024 * 1024),
        cost_estimate=pl.CostEstimate(
            flops=2 * ITERS * 7 * D * D * D // 3, bytes_accessed=D * D * 2, transcendentals=0
        ),
        name="newton_schulz",
    )(place, whole)


def body(grad_parts, momentum_owned, owner_table, step_offset):
    replica, shard = lax.axis_index("dp"), lax.axis_index("shard")
    mats, piece_rows = grad_parts.shape[1], grad_parts.shape[2]
    sub_rows = momentum_owned.shape[2]
    owner_slot = (owner_table + step_offset[0]) % mats
    slot_ids = jnp.arange(mats, dtype=jnp.int32)
    owner_order = jnp.sum(
        jnp.where(owner_slot[None, :] == slot_ids[:, None], slot_ids[None, :], 0), axis=1
    )
    momentum = momentum_owned[0]

    parts = swap(grad_parts[0], "dp")

    by_slot = xor_swap(jnp.take(momentum.astype(jnp.bfloat16), slot_ids ^ shard, axis=0), "shard")
    by_matrix = jnp.take(by_slot, jnp.take(owner_slot, slot_ids ^ replica) ^ shard, axis=0)
    own_momentum = jnp.take(xor_swap(by_matrix, "dp"), slot_ids ^ replica, axis=0).reshape(piece_rows, D)

    summed = lax.optimization_barrier(jnp.sum(parts.astype(jnp.float32), axis=0))
    grad = summed.astype(jnp.bfloat16)
    grad_float = grad.astype(jnp.float32)
    moment_here = momentum_decay * own_momentum.astype(jnp.float32) + grad_float
    nesterov = (grad_float + momentum_decay * moment_here).astype(jnp.bfloat16)
    whole = lax.all_gather(nesterov, "shard", axis=0, tiled=True)

    grad_blocks = swap(grad.reshape(mats, sub_rows, D), "dp")
    grad_rows = swap(jnp.take(grad_blocks, owner_order, axis=0), "shard")
    moment = momentum_decay * momentum + grad_rows.astype(jnp.float32)

    update = newton_schulz(whole, shard.astype(jnp.int32)[None], piece_rows)
    return (update[None], moment[None])


def solution(mesh):
    placed = (P("dp", None, "shard", None), P("shard", None, "dp", None), P(), P())
    return jax.shard_map(
        body,
        mesh=mesh,
        in_specs=placed,
        out_specs=(P("dp", "shard", None), P("shard", None, "dp", None)),
        check_vma=False,
    )
```

```python
import jax
import jax.numpy as jnp
from jax import lax
from jax.experimental import pallas as pl
from jax.experimental.pallas import tpu as pltpu
from jax.sharding import PartitionSpec as P

D = 1536
ITERS = 2
TILE = 512

momentum_decay = 0.95
linear_coef = 3.4445
cubic_coef = -4.775
quintic_coef = 2.0315


def swap(value, axis):
    return lax.all_to_all(value, axis, split_axis=0, concat_axis=0, tiled=True)


def shift(value, axis, by):
    count = lax.axis_size(axis)
    return lax.ppermute(value, axis, [(i, (i + by) % count) for i in range(count)])


def core_swap(value):
    return lax.ppermute(value, "core", [(0, 1), (1, 0)])


def after(value, other):
    return lax.optimization_barrier((value, other))


def spread_sums(picks, axes):
    places = [lax.axis_index(axis) for axis in axes]
    counts = [lax.axis_size(axis) for axis in axes]
    target = [
        lambda by, pick=pick, place=place, count=count: pick(lax.rem(place + by, count))
        for pick, place, count in zip(picks, places, counts)
    ]
    near = [
        [shift(block(1), axis, 1), shift(block(count - 1), axis, -1)]
        for block, axis, count in zip(target, axes, counts)
    ]
    far = []
    for n, (block, axis) in enumerate(zip(target, axes)):
        sent, near[n][0] = after(block(2), near[n][0])
        far.append(shift(sent, axis, 2))
    totals = []
    for n, block in enumerate(target):
        total = block(0).astype(jnp.float32)
        for part in near[n] + [far[n]]:
            total = total + part.astype(jnp.float32)
        totals.append(total)
    return totals, near[-1][-1]


def ring_gather(piece, axis):
    rows = piece.shape[0]
    forth, back = piece, piece
    pieces = [piece]
    for _ in range(lax.axis_size(axis) // 2 - 1):
        forth, back = shift(forth, axis, 1), shift(back, axis, -1)
        pieces += [forth, back]
    return pieces + [shift(forth[: rows // 2], axis, 1), shift(back[rows // 2 :], axis, -1)]


def newton_schulz_kernel(*refs):
    scratch = 8
    pieces, out_ref = refs[: -scratch - 1], refs[-scratch - 1]
    first_ref, later_ref, gram_ref, poly_ref, kept_ref, diag_ref, square_ref, sems = refs[-scratch:]
    tiles = D // TILE
    contract_last = (((1,), (1,)), ((), ()))
    copies, start = [], 0
    for n, piece in enumerate(pieces):
        height = piece.shape[0]
        copies.append(pltpu.make_async_copy(piece, first_ref.at[pl.ds(start, height), :], sems.at[n]))
        start += height
    for copy in copies:
        copy.start()
    diag_ref[...] = jnp.zeros_like(diag_ref)
    square_ref[...] = jnp.zeros_like(square_ref)
    for copy in copies:
        copy.wait()

    def span(start, size):
        return pl.ds(pl.multiple_of(start, 256), size)

    def symmetric(product, finish, target):
        def step(t, carry):
            i = (t >= 2).astype(jnp.int32) * TILE
            j = (1 + (t >= 1).astype(jnp.int32)) * TILE
            k = t * TILE
            small = TILE // 2
            for row, column, height, diagonal in (
                (i, j, TILE, False),
                (i, j + small, TILE, False),
                (k, k, TILE, True),
                (k + small, k + small, small, True),
            ):
                low = finish(row, column, height, diagonal, product(row, column, height))
                target[span(row, height), span(column, small)] = low
                if not diagonal:
                    target[span(column, small), span(row, height)] = low.T
                elif height == TILE:
                    target[span(column, small), span(row + small, small)] = low[small:, :].T
            return carry

        lax.fori_loop(0, tiles, step, 0, unroll=True)

    def sweep(source, store, measured):
        def gram_product(row, column, height):
            return lax.dot_general(
                source[span(row, height), :],
                source[span(column, TILE // 2), :],
                contract_last,
                preferred_element_type=jnp.float32,
            )

        def gram_finish(row, column, height, diagonal, total):
            if measured and diagonal:
                rows = lax.broadcasted_iota(jnp.int32, total.shape, 0)
                columns = lax.broadcasted_iota(jnp.int32, total.shape, 1)
                diag_ref[...] += jnp.sum(jnp.where(rows == columns, total, 0.0), axis=0, keepdims=True)
            return total.astype(jnp.bfloat16)

        symmetric(gram_product, gram_finish, gram_ref)
        if measured:
            inverse = 1.0 / (jnp.sqrt(jnp.sum(diag_ref[...])) + 1e-07)
            cubic = cubic_coef * (inverse * inverse)
            quintic = quintic_coef * (inverse * inverse) * (inverse * inverse)
        else:
            inverse, cubic, quintic = 1.0, cubic_coef, quintic_coef

        def poly_product(row, column, height):
            return jnp.dot(
                gram_ref[span(row, height), :], gram_ref[:, span(column, TILE // 2)], preferred_element_type=jnp.float32
            )

        def poly_finish(row, column, height, diagonal, total):
            gram = gram_ref[span(row, height), span(column, TILE // 2)].astype(jnp.float32)
            return (cubic * gram + quintic * total).astype(jnp.bfloat16)

        symmetric(poly_product, poly_finish, poly_ref)

        def mix_tile(t, carry):
            rows = span(t * TILE, TILE)
            for c in range(0, D, TILE // 2):
                columns = slice(c, c + TILE // 2)
                total = jnp.dot(poly_ref[rows, :], source[:, columns], preferred_element_type=jnp.float32)
                store(t, rows, columns, (linear_coef * source[rows, columns].astype(jnp.float32) + total) * inverse)
            return carry

        lax.fori_loop(0, tiles, mix_tile, 0, unroll=True)

    def store_later(t, rows, columns, mixed):
        later_ref[rows, columns] = mixed.astype(jnp.bfloat16)

    def store_mixed(t, rows, columns, mixed):
        kept_ref[t, :, columns] = mixed[: kept_ref.shape[1], :]
        square_ref[:, columns] += jnp.sum(mixed * mixed, axis=0, keepdims=True)

    sweep(first_ref, store_later, True)
    sweep(later_ref, store_mixed, False)
    scale = lax.rsqrt(jnp.sum(square_ref[...]) / (D * D) + 1e-06)
    out_ref[...] = (kept_ref[0] * scale).astype(jnp.bfloat16)


def newton_schulz(pieces, rows):
    return pl.pallas_call(
        newton_schulz_kernel,
        out_shape=jax.ShapeDtypeStruct((rows, D), jnp.bfloat16),
        in_specs=[pl.BlockSpec(memory_space=pl.ANY)] * len(pieces),
        out_specs=pl.BlockSpec(memory_space=pltpu.VMEM),
        scratch_shapes=[
            pltpu.VMEM((D, D), jnp.bfloat16),
            pltpu.VMEM((D, D), jnp.bfloat16),
            pltpu.VMEM((D, D), jnp.bfloat16),
            pltpu.VMEM((D, D), jnp.bfloat16),
            pltpu.VMEM((D // TILE, rows, D), jnp.float32),
            pltpu.VMEM((1, TILE // 2), jnp.float32),
            pltpu.VMEM((1, D), jnp.float32),
            pltpu.SemaphoreType.DMA((len(pieces),)),
        ],
        compiler_params=pltpu.CompilerParams(vmem_limit_bytes=40 * 1024 * 1024),
        cost_estimate=pl.CostEstimate(
            flops=2 * ITERS * 7 * D * D * D // 3, bytes_accessed=D * D * 2, transcendentals=0
        ),
        name="newton_schulz",
    )(*pieces)


def body(grad_parts, momentum_owned, owner_table, step_offset):
    replicas, shards = ("y", "x"), ("z", "core")
    mats, piece_rows = grad_parts.shape[1], grad_parts.shape[2]
    sub_rows = momentum_owned.shape[2]
    owner_slot = (owner_table + step_offset[0]) % mats
    slot_ids = jnp.arange(mats, dtype=jnp.int32)
    owner_order = jnp.sum(
        jnp.where(owner_slot[None, :] == slot_ids[:, None], slot_ids[None, :], 0), axis=1
    )
    momentum = momentum_owned[0]

    tall, across = lax.axis_size("y"), lax.axis_size("x")
    parts = grad_parts.reshape(tall, across, piece_rows, D)
    half = piece_rows // 2

    def upper_for(t):
        return lax.dynamic_slice(parts, (0, t, 0, 0), (tall, 1, half, D)).reshape(tall, half, D)

    def lower_for(t):
        return lax.dynamic_slice(parts, (t, 0, half, 0), (1, across, half, D)).reshape(across, half, D)

    (upper, lower), arrived = spread_sums([upper_for, lower_for], ["x", "y"])
    (upper, lower), _ = spread_sums(
        [lambda t: lax.dynamic_index_in_dim(upper, t, 0, False), lambda t: lax.dynamic_index_in_dim(lower, t, 0, False)],
        ["y", "x"],
    )
    summed = lax.optimization_barrier(jnp.concatenate([upper, lower], axis=0))
    grad = summed.astype(jnp.bfloat16)

    by_slot, _ = after(swap(momentum.astype(jnp.bfloat16), shards), arrived)
    own_momentum = swap(jnp.take(by_slot, owner_slot, axis=0), replicas).reshape(piece_rows, D)

    grad_float = grad.astype(jnp.float32)
    moment_here = momentum_decay * own_momentum.astype(jnp.float32) + grad_float
    nesterov = (grad_float + momentum_decay * moment_here).astype(jnp.bfloat16)
    pieces = ring_gather(nesterov, "z")
    both = pieces + [core_swap(piece) for piece in pieces]

    grad_blocks = swap(grad.reshape(mats, sub_rows, D), replicas)
    grad_blocks, _ = after(grad_blocks, pieces[-3])
    grad_rows = swap(jnp.take(grad_blocks, owner_order, axis=0), shards)
    moment = momentum_decay * momentum + grad_rows.astype(jnp.float32)

    update = newton_schulz(both, piece_rows)
    return (update[None], moment[None])


def solution(mesh):
    fine = jax.sharding.Mesh(mesh.devices.reshape(4, 4, 8, 2), ("y", "x", "z", "core"))
    replicas, shards = ("y", "x"), ("z", "core")
    placed = (P(replicas, None, shards, None), P(shards, None, replicas, None), P(), P())
    return jax.shard_map(
        body,
        mesh=fine,
        in_specs=placed,
        out_specs=(P(replicas, shards, None), P(shards, None, replicas, None)),
        check_vma=False,
    )
```

```python
import jax
import jax.numpy as jnp
from jax import lax
from jax.experimental import pallas as pl
from jax.experimental.pallas import tpu as pltpu
from jax.sharding import PartitionSpec as P

D = 1536
ITERS = 2
TILE = 512

momentum_decay = 0.95
linear_coef = 3.4445
cubic_coef = -4.775
quintic_coef = 2.0315


def swap(value, axis):
    return lax.all_to_all(value, axis, split_axis=0, concat_axis=0, tiled=True)


def shift(value, axis, by):
    count = lax.axis_size(axis)
    return lax.ppermute(value, axis, [(i, (i + by) % count) for i in range(count)])


def core_swap(value):
    return lax.ppermute(value, "core", [(0, 1), (1, 0)])


def pick_blocks(blocks, order):
    return blocks.at[order].get(mode="promise_in_bounds")


def after(value, other):
    return lax.optimization_barrier((value, other))


def spread_sums(picks, axes):
    places = [lax.axis_index(axis) for axis in axes]
    counts = [lax.axis_size(axis) for axis in axes]
    target = [
        lambda by, pick=pick, place=place, count=count: pick(lax.rem(place + by, count))
        for pick, place, count in zip(picks, places, counts)
    ]
    near = [
        [shift(block(1), axis, 1), shift(block(count - 1), axis, -1)]
        for block, axis, count in zip(target, axes, counts)
    ]
    far = []
    for n, (block, axis) in enumerate(zip(target, axes)):
        sent = block(2)
        if n > 0:
            sent, near[n][0] = after(sent, near[n][0])
        far.append(shift(sent, axis, 2))
    totals = []
    for n, block in enumerate(target):
        total = block(0).astype(jnp.float32)
        for part in near[n] + [far[n]]:
            total = total + part.astype(jnp.float32)
        totals.append(total)
    return totals, near[-1][-1]


def ring_gather(piece, axis):
    rows = piece.shape[0]
    forth, back = piece, piece
    pieces = [piece]
    for _ in range(lax.axis_size(axis) // 2 - 1):
        forth, back = shift(forth, axis, 1), shift(back, axis, -1)
        pieces += [forth, back]
    return pieces + [shift(forth[: rows // 2], axis, 1), shift(back[rows // 2 :], axis, -1)]


def newton_schulz_kernel(*refs):
    scratch = 8
    pieces, out_ref = refs[: -scratch - 1], refs[-scratch - 1]
    first_ref, later_ref, gram_ref, poly_ref, kept_ref, diag_ref, square_ref, sems = refs[-scratch:]
    tiles = D // TILE
    contract_last = (((1,), (1,)), ((), ()))
    copies, start = [], 0
    for n, piece in enumerate(pieces):
        height = piece.shape[0]
        copies.append(pltpu.make_async_copy(piece, first_ref.at[pl.ds(start, height), :], sems.at[n]))
        start += height
    for copy in copies:
        copy.start()
    diag_ref[...] = jnp.zeros_like(diag_ref)
    square_ref[...] = jnp.zeros_like(square_ref)
    for copy in copies:
        copy.wait()

    def span(start, size):
        return pl.ds(pl.multiple_of(start, 256), size)

    def symmetric(product, finish, target):
        def step(t, carry):
            i = (t >= 2).astype(jnp.int32) * TILE
            j = (1 + (t >= 1).astype(jnp.int32)) * TILE
            k = t * TILE
            small = TILE // 2
            for row, column, height, diagonal in (
                (i, j, TILE, False),
                (i, j + small, TILE, False),
                (k, k, TILE, True),
                (k + small, k + small, small, True),
            ):
                low = finish(row, column, height, diagonal, product(row, column, height))
                target[span(row, height), span(column, small)] = low
                if not diagonal:
                    target[span(column, small), span(row, height)] = low.T
                elif height == TILE:
                    target[span(column, small), span(row + small, small)] = low[small:, :].T
            return carry

        lax.fori_loop(0, tiles, step, 0, unroll=True)

    def sweep(source, store, measured):
        def gram_product(row, column, height):
            return lax.dot_general(
                source[span(row, height), :],
                source[span(column, TILE // 2), :],
                contract_last,
                preferred_element_type=jnp.float32,
            )

        def gram_finish(row, column, height, diagonal, total):
            if measured and diagonal:
                rows = lax.broadcasted_iota(jnp.int32, total.shape, 0)
                columns = lax.broadcasted_iota(jnp.int32, total.shape, 1)
                diag_ref[...] += jnp.sum(jnp.where(rows == columns, total, 0.0), axis=0, keepdims=True)
            return total.astype(jnp.bfloat16)

        symmetric(gram_product, gram_finish, gram_ref)
        if measured:
            inverse = 1.0 / (jnp.sqrt(jnp.sum(diag_ref[...])) + 1e-07)
            cubic = cubic_coef * (inverse * inverse)
            quintic = quintic_coef * (inverse * inverse) * (inverse * inverse)
        else:
            inverse, cubic, quintic = 1.0, cubic_coef, quintic_coef

        def poly_product(row, column, height):
            return jnp.dot(
                gram_ref[span(row, height), :], gram_ref[:, span(column, TILE // 2)], preferred_element_type=jnp.float32
            )

        def poly_finish(row, column, height, diagonal, total):
            gram = gram_ref[span(row, height), span(column, TILE // 2)].astype(jnp.float32)
            return (cubic * gram + quintic * total).astype(jnp.bfloat16)

        symmetric(poly_product, poly_finish, poly_ref)

        def mix_tile(t, carry):
            rows = span(t * TILE, TILE)
            for c in range(0, D, TILE // 2):
                columns = slice(c, c + TILE // 2)
                total = jnp.dot(poly_ref[rows, :], source[:, columns], preferred_element_type=jnp.float32)
                store(t, rows, columns, (linear_coef * source[rows, columns].astype(jnp.float32) + total) * inverse)
            return carry

        lax.fori_loop(0, tiles, mix_tile, 0, unroll=True)

    def store_later(t, rows, columns, mixed):
        later_ref[rows, columns] = mixed.astype(jnp.bfloat16)

    def store_mixed(t, rows, columns, mixed):
        kept_ref[t, :, columns] = mixed[: kept_ref.shape[1], :]
        square_ref[:, columns] += jnp.sum(mixed * mixed, axis=0, keepdims=True)

    sweep(first_ref, store_later, True)
    sweep(later_ref, store_mixed, False)
    scale = lax.rsqrt(jnp.sum(square_ref[...]) / (D * D) + 1e-06)
    out_ref[...] = (kept_ref[0] * scale).astype(jnp.bfloat16)


def newton_schulz(pieces, rows):
    return pl.pallas_call(
        newton_schulz_kernel,
        out_shape=jax.ShapeDtypeStruct((rows, D), jnp.bfloat16),
        in_specs=[pl.BlockSpec(memory_space=pl.ANY)] * len(pieces),
        out_specs=pl.BlockSpec(memory_space=pltpu.VMEM),
        scratch_shapes=[
            pltpu.VMEM((D, D), jnp.bfloat16),
            pltpu.VMEM((D, D), jnp.bfloat16),
            pltpu.VMEM((D, D), jnp.bfloat16),
            pltpu.VMEM((D, D), jnp.bfloat16),
            pltpu.VMEM((D // TILE, rows, D), jnp.float32),
            pltpu.VMEM((1, TILE // 2), jnp.float32),
            pltpu.VMEM((1, D), jnp.float32),
            pltpu.SemaphoreType.DMA((len(pieces),)),
        ],
        compiler_params=pltpu.CompilerParams(vmem_limit_bytes=40 * 1024 * 1024),
        cost_estimate=pl.CostEstimate(
            flops=0, bytes_accessed=D * D * 2, transcendentals=0
        ),
        name="newton_schulz",
    )(*pieces)


def body(grad_parts, momentum_owned, owner_table, step_offset):
    replicas, shards = ("y", "x"), ("z", "core")
    mats, piece_rows = grad_parts.shape[1], grad_parts.shape[2]
    sub_rows = momentum_owned.shape[2]
    owner_slot = (owner_table + step_offset[0]) % mats
    slot_ids = jnp.arange(mats, dtype=jnp.int32)
    owner_order = jnp.sum(
        jnp.where(owner_slot[None, :] == slot_ids[:, None], slot_ids[None, :], 0), axis=1
    )
    momentum = momentum_owned[0]

    tall, across = lax.axis_size("y"), lax.axis_size("x")
    parts = grad_parts.reshape(tall, across, piece_rows, D)
    half = piece_rows // 2

    def upper_for(t):
        return lax.dynamic_slice(parts, (0, t, 0, 0), (tall, 1, half, D)).reshape(tall, half, D)

    def lower_for(t):
        return lax.dynamic_slice(parts, (t, 0, half, 0), (1, across, half, D)).reshape(across, half, D)

    (upper, lower), _ = spread_sums([upper_for, lower_for], ["x", "y"])
    (upper, lower), arrived = spread_sums(
        [lambda t: lax.dynamic_index_in_dim(upper, t, 0, False), lambda t: lax.dynamic_index_in_dim(lower, t, 0, False)],
        ["y", "x"],
    )
    summed = lax.optimization_barrier(jnp.concatenate([upper, lower], axis=0))
    grad = summed.astype(jnp.bfloat16)

    by_slot, _ = after(swap(momentum.astype(jnp.bfloat16), shards), arrived)
    own_momentum = swap(pick_blocks(by_slot, owner_slot), replicas).reshape(piece_rows, D)

    grad_float = grad.astype(jnp.float32)
    moment_here = momentum_decay * own_momentum.astype(jnp.float32) + grad_float
    nesterov = (grad_float + momentum_decay * moment_here).astype(jnp.bfloat16)
    pieces = ring_gather(nesterov, "z")
    both = pieces + [core_swap(piece) for piece in pieces]

    grad_blocks = swap(grad.reshape(mats, sub_rows, D), replicas)
    grad_blocks, _ = after(grad_blocks, pieces[-3])
    grad_rows = swap(pick_blocks(grad_blocks, owner_order), shards)
    moment = momentum_decay * momentum + grad_rows.astype(jnp.float32)

    update = newton_schulz(both, piece_rows)
    return (update[None], moment[None])


def solution(mesh):
    fine = jax.sharding.Mesh(mesh.devices.reshape(4, 4, 8, 2), ("y", "x", "z", "core"))
    replicas, shards = ("y", "x"), ("z", "core")
    placed = (P(replicas, None, shards, None), P(shards, None, replicas, None), P(), P())
    return jax.shard_map(
        body,
        mesh=fine,
        in_specs=placed,
        out_specs=(P(replicas, shards, None), P(shards, None, replicas, None)),
        check_vma=False,
    )
```

```python
import jax
import jax.numpy as jnp
from jax import lax
from jax.experimental import pallas as pl
from jax.experimental.pallas import tpu as pltpu
from jax.sharding import PartitionSpec as P

D = 1536
ITERS = 2
TILE = 512

momentum_decay = 0.95
linear_coef = 3.4445
cubic_coef = -4.775
quintic_coef = 2.0315


def swap(value, axis):
    return lax.all_to_all(value, axis, split_axis=0, concat_axis=0, tiled=True)


def shift(value, axis, by):
    count = lax.axis_size(axis)
    return lax.ppermute(value, axis, [(i, (i + by) % count) for i in range(count)])


def core_swap(value):
    return lax.ppermute(value, "core", [(0, 1), (1, 0)])


def pick_blocks(blocks, order):
    return blocks.at[order].get(mode="promise_in_bounds")


def after(value, other):
    return lax.optimization_barrier((value, other))


def spread_sums(picks, axes):
    places = [lax.axis_index(axis) for axis in axes]
    counts = [lax.axis_size(axis) for axis in axes]
    target = [
        lambda by, pick=pick, place=place, count=count: pick(lax.rem(place + by, count))
        for pick, place, count in zip(picks, places, counts)
    ]
    near = [
        [shift(block(1), axis, 1), shift(block(count - 1), axis, -1)]
        for block, axis, count in zip(target, axes, counts)
    ]
    far = []
    for n, (block, axis) in enumerate(zip(target, axes)):
        sent = block(2)
        if n > 0:
            sent, near[n][0] = after(sent, near[n][0])
        far.append(shift(sent, axis, 2))
    totals = []
    for n, block in enumerate(target):
        total = block(0).astype(jnp.float32)
        for part in near[n] + [far[n]]:
            total = total + part.astype(jnp.float32)
        totals.append(total)
    return totals, near[-1][0]


def ring_gather(piece, axis):
    rows = piece.shape[0]
    forth, back = piece, piece
    pieces = [piece]
    for _ in range(lax.axis_size(axis) // 2 - 1):
        forth, back = shift(forth, axis, 1), shift(back, axis, -1)
        pieces += [forth, back]
    return pieces + [shift(forth[: rows // 2], axis, 1), shift(back[rows // 2 :], axis, -1)]


def newton_schulz_kernel(*refs):
    scratch = 8
    pieces, out_ref = refs[: -scratch - 1], refs[-scratch - 1]
    first_ref, later_ref, gram_ref, poly_ref, kept_ref, diag_ref, square_ref, sems = refs[-scratch:]
    tiles = D // TILE
    small = TILE // 2
    contract_last = (((1,), (1,)), ((), ()))
    copies, start = [], 0
    for n, piece in enumerate(pieces):
        height = piece.shape[0]
        copies.append(pltpu.make_async_copy(piece, first_ref.at[pl.ds(start, height), :], sems.at[n]))
        start += height
    for copy in copies:
        copy.start()
    for copy in copies:
        copy.wait()

    def symmetric(product, finish):
        for t in range(tiles):
            i, j = ((0, 1), (0, 2), (1, 2))[t]
            for row, column, height, diagonal in (
                (i * TILE, j * TILE, TILE, False),
                (i * TILE, j * TILE + small, TILE, False),
                (t * TILE, t * TILE, TILE, True),
                (t * TILE + small, t * TILE + small, small, True),
            ):
                rows, columns = slice(row, row + height), slice(column, column + small)
                finish(rows, columns, diagonal, product(rows, columns))

    def store(target, rows, columns, diagonal, low):
        target[rows, columns] = low
        if not diagonal:
            target[columns, rows] = low.T
        elif rows.stop - rows.start == TILE:
            target[columns, rows.start + small : rows.stop] = low[small:, :].T

    def gram(source, measured):
        def product(rows, columns):
            return lax.dot_general(
                source[rows, :], source[columns, :], contract_last, preferred_element_type=jnp.float32
            )

        def finish(rows, columns, diagonal, total):
            if measured and diagonal:
                down = lax.broadcasted_iota(jnp.int32, total.shape, 0)
                along = lax.broadcasted_iota(jnp.int32, total.shape, 1)
                diag_ref[...] += jnp.sum(jnp.where(down == along, total, 0.0), axis=0, keepdims=True)
            store(gram_ref, rows, columns, diagonal, total.astype(jnp.bfloat16))

        symmetric(product, finish)

    def poly(cubic, quintic):
        def product(rows, columns):
            return jnp.dot(gram_ref[rows, :], gram_ref[:, columns], preferred_element_type=jnp.float32)

        def finish(rows, columns, diagonal, total):
            value = cubic * gram_ref[rows, columns].astype(jnp.float32) + quintic * total
            store(poly_ref, rows, columns, diagonal, value.astype(jnp.bfloat16))

        symmetric(product, finish)

    def mix(source, finish):
        for t in range(tiles):
            rows = slice(t * TILE, (t + 1) * TILE)
            for c in range(0, D, small):
                columns = slice(c, c + small)
                total = jnp.dot(poly_ref[rows, :], source[:, columns], preferred_element_type=jnp.float32)
                finish(rows, columns, linear_coef * source[rows, columns].astype(jnp.float32) + total)

    diag_ref[...] = jnp.zeros_like(diag_ref)
    gram(first_ref, True)
    inverse = 1.0 / (jnp.sqrt(jnp.sum(diag_ref[...])) + 1e-07)
    poly(cubic_coef * (inverse * inverse), quintic_coef * (inverse * inverse) * (inverse * inverse))

    def keep_all(rows, columns, mixed):
        later_ref[rows, columns] = (mixed * inverse).astype(jnp.bfloat16)

    mix(first_ref, keep_all)

    square_ref[...] = jnp.zeros_like(square_ref)
    gram(later_ref, False)
    poly(cubic_coef, quintic_coef)

    def keep_first(rows, columns, mixed):
        if rows.start == 0:
            kept_ref[:, columns] = mixed[: kept_ref.shape[0], :]
        square_ref[...] += jnp.sum(mixed * mixed, axis=0, keepdims=True)

    mix(later_ref, keep_first)
    scale = lax.rsqrt(jnp.sum(square_ref[...]) / (D * D) + 1e-06)
    out_ref[...] = (kept_ref[...] * scale).astype(jnp.bfloat16)


def newton_schulz(pieces, rows):
    return pl.pallas_call(
        newton_schulz_kernel,
        out_shape=jax.ShapeDtypeStruct((rows, D), jnp.bfloat16),
        in_specs=[pl.BlockSpec(memory_space=pl.ANY)] * len(pieces),
        out_specs=pl.BlockSpec(memory_space=pltpu.VMEM),
        scratch_shapes=[
            pltpu.VMEM((D, D), jnp.bfloat16),
            pltpu.VMEM((D, D), jnp.bfloat16),
            pltpu.VMEM((D, D), jnp.bfloat16),
            pltpu.VMEM((D, D), jnp.bfloat16),
            pltpu.VMEM((rows, D), jnp.float32),
            pltpu.VMEM((1, TILE // 2), jnp.float32),
            pltpu.VMEM((1, TILE // 2), jnp.float32),
            pltpu.SemaphoreType.DMA((len(pieces),)),
        ],
        compiler_params=pltpu.CompilerParams(vmem_limit_bytes=40 * 1024 * 1024),
        cost_estimate=pl.CostEstimate(
            flops=2 * ITERS * 7 * D * D * D // 3, bytes_accessed=D * D * 2, transcendentals=0
        ),
        name="newton_schulz",
    )(*pieces)


def body(grad_parts, momentum_owned, owner_table, step_offset):
    replicas, shards = ("y", "x"), ("z", "core")
    mats, piece_rows = grad_parts.shape[1], grad_parts.shape[2]
    sub_rows = momentum_owned.shape[2]
    owner_slot = (owner_table + step_offset[0]) % mats
    slot_ids = jnp.arange(mats, dtype=jnp.int32)
    owner_order = jnp.sum(
        jnp.where(owner_slot[None, :] == slot_ids[:, None], slot_ids[None, :], 0), axis=1
    )
    momentum = momentum_owned[0]

    tall, across = lax.axis_size("y"), lax.axis_size("x")
    parts = grad_parts.reshape(tall, across, piece_rows, D)
    half = piece_rows // 2

    def upper_for(t):
        return lax.dynamic_slice(parts, (0, t, 0, 0), (tall, 1, half, D)).reshape(tall, half, D)

    def lower_for(t):
        return lax.dynamic_slice(parts, (t, 0, half, 0), (1, across, half, D)).reshape(across, half, D)

    (upper, lower), _ = spread_sums([upper_for, lower_for], ["x", "y"])
    (upper, lower), arrived = spread_sums(
        [lambda t: lax.dynamic_index_in_dim(upper, t, 0, False), lambda t: lax.dynamic_index_in_dim(lower, t, 0, False)],
        ["y", "x"],
    )
    summed = lax.optimization_barrier(jnp.concatenate([upper, lower], axis=0))
    grad = summed.astype(jnp.bfloat16)

    by_slot, _ = after(swap(momentum.astype(jnp.bfloat16), shards), arrived)
    own_momentum = swap(pick_blocks(by_slot, owner_slot), replicas).reshape(piece_rows, D)

    grad_float = grad.astype(jnp.float32)
    moment_here = momentum_decay * own_momentum.astype(jnp.float32) + grad_float
    nesterov = (grad_float + momentum_decay * moment_here).astype(jnp.bfloat16)
    pieces = ring_gather(nesterov, "z")
    both = pieces + [core_swap(piece) for piece in pieces]

    grad_blocks = swap(grad.reshape(mats, sub_rows, D), replicas)
    grad_blocks, _ = after(grad_blocks, pieces[-3])
    grad_rows = swap(pick_blocks(grad_blocks, owner_order), shards)
    moment = momentum_decay * momentum + grad_rows.astype(jnp.float32)

    update = newton_schulz(both, piece_rows)
    return (update[None], moment[None])


def solution(mesh):
    fine = jax.sharding.Mesh(mesh.devices.reshape(4, 4, 8, 2), ("y", "x", "z", "core"))
    replicas, shards = ("y", "x"), ("z", "core")
    placed = (P(replicas, None, shards, None), P(shards, None, replicas, None), P(), P())
    return jax.shard_map(
        body,
        mesh=fine,
        in_specs=placed,
        out_specs=(P(replicas, shards, None), P(shards, None, replicas, None)),
        check_vma=False,
    )
```

```python
import jax
import jax.numpy as jnp
from jax import lax
from jax.experimental import pallas as pl
from jax.experimental.pallas import tpu as pltpu
from jax.sharding import PartitionSpec as P

D = 1536
ITERS = 2
TILE = 512

momentum_decay = 0.95
linear_coef = 3.4445
cubic_coef = -4.775
quintic_coef = 2.0315


def swap(value, axis):
    return lax.all_to_all(value, axis, split_axis=0, concat_axis=0, tiled=True)


def shift(value, axis, by):
    count = lax.axis_size(axis)
    return lax.ppermute(value, axis, [(i, (i + by) % count) for i in range(count)])


def core_swap(value):
    return lax.ppermute(value, "core", [(0, 1), (1, 0)])


def pick_blocks(blocks, order):
    return blocks.at[order].get(mode="promise_in_bounds")


def after(value, other):
    return lax.optimization_barrier((value, other))


def spread_sums(picks, axes):
    places = [lax.axis_index(axis) for axis in axes]
    counts = [lax.axis_size(axis) for axis in axes]
    target = [
        lambda by, pick=pick, place=place, count=count: pick(lax.rem(place + by, count))
        for pick, place, count in zip(picks, places, counts)
    ]
    near = [
        [shift(block(1), axis, 1), shift(block(count - 1), axis, -1)]
        for block, axis, count in zip(target, axes, counts)
    ]
    far = []
    for n, (block, axis) in enumerate(zip(target, axes)):
        sent = block(2)
        if n > 0:
            sent, near[n][0] = after(sent, near[n][0])
        far.append(shift(sent, axis, 2))
    totals = []
    for n, block in enumerate(target):
        total = block(0).astype(jnp.float32)
        for part in near[n] + [far[n]]:
            total = total + part.astype(jnp.float32)
        totals.append(total)
    return totals, near[-1][0]


def ring_gather(piece, axis):
    rows = piece.shape[0]
    forth, back = piece, piece
    pieces = [piece]
    for _ in range(lax.axis_size(axis) // 2 - 1):
        forth, back = shift(forth, axis, 1), shift(back, axis, -1)
        pieces += [forth, back]
    return pieces + [shift(forth[: rows // 2], axis, 1), shift(back[rows // 2 :], axis, -1)]


def newton_schulz_kernel(*refs):
    scratch = 8
    pieces, out_ref = refs[: -scratch - 1], refs[-scratch - 1]
    first_ref, later_ref, gram_ref, poly_ref, kept_ref, diag_ref, square_ref, sems = refs[-scratch:]
    tiles = D // TILE
    contract_last = (((1,), (1,)), ((), ()))
    copies, start = [], 0
    for n, piece in enumerate(pieces):
        height = piece.shape[0]
        copies.append(pltpu.make_async_copy(piece, first_ref.at[pl.ds(start, height), :], sems.at[n]))
        start += height
    for copy in copies:
        copy.start()
    diag_ref[...] = jnp.zeros_like(diag_ref)
    square_ref[...] = jnp.zeros_like(square_ref)
    for copy in copies:
        copy.wait()

    def span(start, size):
        return pl.ds(pl.multiple_of(start, 256), size)

    def symmetric(product, finish, target):
        def step(t, carry):
            i = (t >= 2).astype(jnp.int32) * TILE
            j = (1 + (t >= 1).astype(jnp.int32)) * TILE
            k = t * TILE
            small = TILE // 2
            for row, column, height, diagonal in (
                (i, j, TILE, False),
                (i, j + small, TILE, False),
                (k, k, TILE, True),
                (k + small, k + small, small, True),
            ):
                low = finish(row, column, height, diagonal, product(row, column, height))
                target[span(row, height), span(column, small)] = low
                if not diagonal:
                    target[span(column, small), span(row, height)] = low.T
                elif height == TILE:
                    target[span(column, small), span(row + small, small)] = low[small:, :].T
            return carry

        lax.fori_loop(0, tiles, step, 0)

    def sweep(source, store, measured):
        def gram_product(row, column, height):
            return lax.dot_general(
                source[span(row, height), :],
                source[span(column, TILE // 2), :],
                contract_last,
                preferred_element_type=jnp.float32,
            )

        def gram_finish(row, column, height, diagonal, total):
            if measured and diagonal:
                rows = lax.broadcasted_iota(jnp.int32, total.shape, 0)
                columns = lax.broadcasted_iota(jnp.int32, total.shape, 1)
                diag_ref[...] += jnp.sum(jnp.where(rows == columns, total, 0.0), axis=0, keepdims=True)
            return total.astype(jnp.bfloat16)

        symmetric(gram_product, gram_finish, gram_ref)
        if measured:
            inverse = 1.0 / (jnp.sqrt(jnp.sum(diag_ref[...])) + 1e-07)
            cubic = cubic_coef * (inverse * inverse)
            quintic = quintic_coef * (inverse * inverse) * (inverse * inverse)
        else:
            inverse, cubic, quintic = 1.0, cubic_coef, quintic_coef

        def poly_product(row, column, height):
            return jnp.dot(
                gram_ref[span(row, height), :], gram_ref[:, span(column, TILE // 2)], preferred_element_type=jnp.float32
            )

        def poly_finish(row, column, height, diagonal, total):
            gram = gram_ref[span(row, height), span(column, TILE // 2)].astype(jnp.float32)
            return (cubic * gram + quintic * total).astype(jnp.bfloat16)

        symmetric(poly_product, poly_finish, poly_ref)

        def mix_tile(t, carry):
            rows = span(t * TILE, TILE)
            for c in range(0, D, TILE // 2):
                columns = slice(c, c + TILE // 2)
                total = jnp.dot(poly_ref[rows, :], source[:, columns], preferred_element_type=jnp.float32)
                store(t, rows, columns, (linear_coef * source[rows, columns].astype(jnp.float32) + total) * inverse)
            return carry

        lax.fori_loop(0, tiles, mix_tile, 0)

    def store_later(t, rows, columns, mixed):
        later_ref[rows, columns] = mixed.astype(jnp.bfloat16)

    def store_mixed(t, rows, columns, mixed):
        kept_ref[t, :, columns] = mixed[: kept_ref.shape[1], :]
        square_ref[:, columns] += jnp.sum(mixed * mixed, axis=0, keepdims=True)

    sweep(first_ref, store_later, True)
    sweep(later_ref, store_mixed, False)
    scale = lax.rsqrt(jnp.sum(square_ref[...]) / (D * D) + 1e-06)
    out_ref[...] = (kept_ref[0] * scale).astype(jnp.bfloat16)


def newton_schulz(pieces, rows):
    return pl.pallas_call(
        newton_schulz_kernel,
        out_shape=jax.ShapeDtypeStruct((rows, D), jnp.bfloat16),
        in_specs=[pl.BlockSpec(memory_space=pl.ANY)] * len(pieces),
        out_specs=pl.BlockSpec(memory_space=pltpu.VMEM),
        scratch_shapes=[
            pltpu.VMEM((D, D), jnp.bfloat16),
            pltpu.VMEM((D, D), jnp.bfloat16),
            pltpu.VMEM((D, D), jnp.bfloat16),
            pltpu.VMEM((D, D), jnp.bfloat16),
            pltpu.VMEM((D // TILE, rows, D), jnp.float32),
            pltpu.VMEM((1, TILE // 2), jnp.float32),
            pltpu.VMEM((1, D), jnp.float32),
            pltpu.SemaphoreType.DMA((len(pieces),)),
        ],
        compiler_params=pltpu.CompilerParams(vmem_limit_bytes=40 * 1024 * 1024),
        cost_estimate=pl.CostEstimate(
            flops=2 * ITERS * 7 * D * D * D // 3, bytes_accessed=D * D * 2, transcendentals=0
        ),
        name="newton_schulz",
    )(*pieces)


def body(grad_parts, momentum_owned, owner_table, step_offset):
    replicas, shards = ("y", "x"), ("z", "core")
    mats, piece_rows = grad_parts.shape[1], grad_parts.shape[2]
    sub_rows = momentum_owned.shape[2]
    owner_slot = (owner_table + step_offset[0]) % mats
    slot_ids = jnp.arange(mats, dtype=jnp.int32)
    owner_order = jnp.sum(
        jnp.where(owner_slot[None, :] == slot_ids[:, None], slot_ids[None, :], 0), axis=1
    )
    momentum = momentum_owned[0]

    tall, across = lax.axis_size("y"), lax.axis_size("x")
    parts = grad_parts.reshape(tall, across, piece_rows, D)
    half = piece_rows // 2

    def upper_for(t):
        return lax.dynamic_slice(parts, (0, t, 0, 0), (tall, 1, half, D)).reshape(tall, half, D)

    def lower_for(t):
        return lax.dynamic_slice(parts, (t, 0, half, 0), (1, across, half, D)).reshape(across, half, D)

    (upper, lower), _ = spread_sums([upper_for, lower_for], ["x", "y"])
    (upper, lower), arrived = spread_sums(
        [lambda t: lax.dynamic_index_in_dim(upper, t, 0, False), lambda t: lax.dynamic_index_in_dim(lower, t, 0, False)],
        ["y", "x"],
    )
    summed = lax.optimization_barrier(jnp.concatenate([upper, lower], axis=0))
    grad = summed.astype(jnp.bfloat16)

    by_slot, _ = after(swap(momentum.astype(jnp.bfloat16), shards), arrived)
    own_momentum = swap(pick_blocks(by_slot, owner_slot), replicas).reshape(piece_rows, D)

    grad_float = grad.astype(jnp.float32)
    moment_here = momentum_decay * own_momentum.astype(jnp.float32) + grad_float
    nesterov = (grad_float + momentum_decay * moment_here).astype(jnp.bfloat16)

    pieces = ring_gather(nesterov, "z")

    grad_blocks = swap(grad.reshape(mats, sub_rows, D), replicas)
    grad_blocks, swap_2 = after(grad_blocks, pieces[3])
    ordered, swap_3 = after(pick_blocks(grad_blocks, owner_order), pieces[5])
    grad_rows = swap(ordered, shards)
    swapped = pieces[:3] + [swap_2, pieces[4], swap_3] + pieces[6:]
    both = pieces + [core_swap(piece) for piece in swapped]
    moment = momentum_decay * momentum + grad_rows.astype(jnp.float32)

    update = newton_schulz(both, piece_rows)
    return (update[None], moment[None])


def solution(mesh):
    fine = jax.sharding.Mesh(mesh.devices.reshape(4, 4, 8, 2), ("y", "x", "z", "core"))
    replicas, shards = ("y", "x"), ("z", "core")
    placed = (P(replicas, None, shards, None), P(shards, None, replicas, None), P(), P())
    return jax.shard_map(
        body,
        mesh=fine,
        in_specs=placed,
        out_specs=(P(replicas, shards, None), P(shards, None, replicas, None)),
        check_vma=False,
    )
```

```python
import jax
import jax.numpy as jnp
from jax import lax
from jax.experimental import pallas as pl
from jax.experimental.pallas import tpu as pltpu
from jax.sharding import PartitionSpec as P

D = 1536
ITERS = 2
TILE = 512

momentum_decay = 0.95
linear_coef = 3.4445
cubic_coef = -4.775
quintic_coef = 2.0315


def swap(value, axis):
    return lax.all_to_all(value, axis, split_axis=0, concat_axis=0, tiled=True)


def shift(value, axis, by):
    count = lax.axis_size(axis)
    return lax.ppermute(value, axis, [(i, (i + by) % count) for i in range(count)])


def core_swap(value):
    return lax.ppermute(value, "core", [(0, 1), (1, 0)])


def pick_blocks(blocks, order):
    return blocks.at[order].get(mode="promise_in_bounds")


def after(value, other):
    return lax.optimization_barrier((value, other))


def spread_sums(picks, axes):
    places = [lax.axis_index(axis) for axis in axes]
    counts = [lax.axis_size(axis) for axis in axes]
    target = [
        lambda by, pick=pick, place=place, count=count: pick(lax.rem(place + by, count))
        for pick, place, count in zip(picks, places, counts)
    ]
    near = [
        [shift(block(1), axis, 1), shift(block(count - 1), axis, -1)]
        for block, axis, count in zip(target, axes, counts)
    ]
    far = []
    for n, (block, axis) in enumerate(zip(target, axes)):
        sent = block(2)
        if n > 0:
            sent, near[n][0] = after(sent, near[n][0])
        far.append(shift(sent, axis, 2))
    totals = []
    for n, block in enumerate(target):
        total = block(0).astype(jnp.float32)
        for part in near[n] + [far[n]]:
            total = total + part.astype(jnp.float32)
        totals.append(total)
    return totals, near[-1][0]


def ring_gather(piece, axis):
    rows = piece.shape[0]
    forth, back = piece, piece
    pieces = [piece]
    for _ in range(lax.axis_size(axis) // 2 - 1):
        forth, back = shift(forth, axis, 1), shift(back, axis, -1)
        pieces += [forth, back]
    return pieces + [shift(forth[: rows // 2], axis, 1), shift(back[rows // 2 :], axis, -1)]


def newton_schulz_kernel(*refs):
    scratch = 8
    pieces, out_ref = refs[: -scratch - 1], refs[-scratch - 1]
    first_ref, later_ref, gram_ref, poly_ref, kept_ref, diag_ref, square_ref, sems = refs[-scratch:]
    tiles = D // TILE
    contract_last = (((1,), (1,)), ((), ()))
    copies, start = [], 0
    for n, piece in enumerate(pieces):
        height = piece.shape[0]
        copies.append(pltpu.make_async_copy(piece, first_ref.at[pl.ds(start, height), :], sems.at[n]))
        start += height
    for copy in copies:
        copy.start()
    diag_ref[...] = jnp.zeros_like(diag_ref)
    square_ref[...] = jnp.zeros_like(square_ref)
    for copy in copies:
        copy.wait()

    def span(start, size):
        return pl.ds(pl.multiple_of(start, 256), size)

    def symmetric(product, finish, target):
        def step(t, carry):
            i = (t >= 2).astype(jnp.int32) * TILE
            j = (1 + (t >= 1).astype(jnp.int32)) * TILE
            k = t * TILE
            small = TILE // 2
            for row, column, height, diagonal in (
                (i, j, TILE, False),
                (i, j + small, TILE, False),
                (k, k, TILE, True),
                (k + small, k + small, small, True),
            ):
                low = finish(row, column, height, diagonal, product(row, column, height))
                target[span(row, height), span(column, small)] = low
                if not diagonal:
                    target[span(column, small), span(row, height)] = low.T
                elif height == TILE:
                    target[span(column, small), span(row + small, small)] = low[small:, :].T
            return carry

        lax.fori_loop(0, tiles, step, 0)

    def sweep(source, store, measured):
        def gram_product(row, column, height):
            return lax.dot_general(
                source[span(row, height), :],
                source[span(column, TILE // 2), :],
                contract_last,
                preferred_element_type=jnp.float32,
            )

        def gram_finish(row, column, height, diagonal, total):
            if measured and diagonal:
                rows = lax.broadcasted_iota(jnp.int32, total.shape, 0)
                columns = lax.broadcasted_iota(jnp.int32, total.shape, 1)
                diag_ref[...] += jnp.sum(jnp.where(rows == columns, total, 0.0), axis=0, keepdims=True)
            return total.astype(jnp.bfloat16)

        symmetric(gram_product, gram_finish, gram_ref)
        if measured:
            inverse = 1.0 / (jnp.sqrt(jnp.sum(diag_ref[...])) + 1e-07)
            cubic = cubic_coef * (inverse * inverse)
            quintic = quintic_coef * (inverse * inverse) * (inverse * inverse)
        else:
            inverse, cubic, quintic = 1.0, cubic_coef, quintic_coef

        def poly_product(row, column, height):
            return jnp.dot(
                gram_ref[span(row, height), :], gram_ref[:, span(column, TILE // 2)], preferred_element_type=jnp.float32
            )

        def poly_finish(row, column, height, diagonal, total):
            gram = gram_ref[span(row, height), span(column, TILE // 2)].astype(jnp.float32)
            return (cubic * gram + quintic * total).astype(jnp.bfloat16)

        symmetric(poly_product, poly_finish, poly_ref)

        def mix_tile(t, carry):
            rows = span(t * TILE, TILE)
            for c in range(0, D, TILE // 2):
                columns = slice(c, c + TILE // 2)
                total = jnp.dot(poly_ref[rows, :], source[:, columns], preferred_element_type=jnp.float32)
                store(t, rows, columns, (linear_coef * source[rows, columns].astype(jnp.float32) + total) * inverse)
            return carry

        lax.fori_loop(0, tiles, mix_tile, 0)

    def store_later(t, rows, columns, mixed):
        later_ref[rows, columns] = mixed.astype(jnp.bfloat16)

    def store_mixed(t, rows, columns, mixed):
        kept_ref[t, :, columns] = mixed[: kept_ref.shape[1], :]
        square_ref[:, columns] += jnp.sum(mixed * mixed, axis=0, keepdims=True)

    sweep(first_ref, store_later, True)
    sweep(later_ref, store_mixed, False)
    scale = lax.rsqrt(jnp.sum(square_ref[...]) / (D * D) + 1e-06)
    out_ref[...] = (kept_ref[0] * scale).astype(jnp.bfloat16)


def newton_schulz(pieces, rows):
    return pl.pallas_call(
        newton_schulz_kernel,
        out_shape=jax.ShapeDtypeStruct((rows, D), jnp.bfloat16),
        in_specs=[pl.BlockSpec(memory_space=pl.ANY)] * len(pieces),
        out_specs=pl.BlockSpec(memory_space=pltpu.VMEM),
        scratch_shapes=[
            pltpu.VMEM((D, D), jnp.bfloat16),
            pltpu.VMEM((D, D), jnp.bfloat16),
            pltpu.VMEM((D, D), jnp.bfloat16),
            pltpu.VMEM((D, D), jnp.bfloat16),
            pltpu.VMEM((D // TILE, rows, D), jnp.float32),
            pltpu.VMEM((1, TILE // 2), jnp.float32),
            pltpu.VMEM((1, D), jnp.float32),
            pltpu.SemaphoreType.DMA((len(pieces),)),
        ],
        compiler_params=pltpu.CompilerParams(vmem_limit_bytes=40 * 1024 * 1024),
        cost_estimate=pl.CostEstimate(
            flops=2 * ITERS * 7 * D * D * D // 3, bytes_accessed=D * D * 2, transcendentals=0
        ),
        name="newton_schulz",
    )(*pieces)


def body(grad_parts, momentum_owned, owner_table, step_offset):
    replicas, shards = ("y", "x"), ("z", "core")
    mats, piece_rows = grad_parts.shape[1], grad_parts.shape[2]
    sub_rows = momentum_owned.shape[2]
    owner_slot = (owner_table + step_offset[0]) % mats
    slot_ids = jnp.arange(mats, dtype=jnp.int32)
    owner_order = jnp.sum(
        jnp.where(owner_slot[None, :] == slot_ids[:, None], slot_ids[None, :], 0), axis=1
    )
    momentum = momentum_owned[0]

    tall, across = lax.axis_size("y"), lax.axis_size("x")
    parts = grad_parts.reshape(tall, across, piece_rows, D)
    half = piece_rows // 2

    def upper_for(t):
        return lax.dynamic_slice(parts, (0, t, 0, 0), (tall, 1, half, D)).reshape(tall, half, D)

    def lower_for(t):
        return lax.dynamic_slice(parts, (t, 0, half, 0), (1, across, half, D)).reshape(across, half, D)

    (upper, lower), _ = spread_sums([upper_for, lower_for], ["x", "y"])
    (upper, lower), arrived = spread_sums(
        [lambda t: lax.dynamic_index_in_dim(upper, t, 0, False), lambda t: lax.dynamic_index_in_dim(lower, t, 0, False)],
        ["y", "x"],
    )
    summed = lax.optimization_barrier(jnp.concatenate([upper, lower], axis=0))
    grad = summed.astype(jnp.bfloat16)

    by_slot, _ = after(swap(momentum.astype(jnp.bfloat16), shards), arrived)
    own_momentum = swap(pick_blocks(by_slot, owner_slot), replicas).reshape(piece_rows, D)

    grad_float = grad.astype(jnp.float32)
    moment_here = momentum_decay * own_momentum.astype(jnp.float32) + grad_float
    nesterov = (grad_float + momentum_decay * moment_here).astype(jnp.bfloat16)

    pieces = ring_gather(nesterov, "z")
    both = pieces + [core_swap(piece) for piece in pieces]

    grad_blocks = swap(grad.reshape(mats, sub_rows, D), replicas)
    grad_blocks, _ = after(grad_blocks, pieces[-3])
    grad_rows = swap(jnp.take(grad_blocks, owner_order, axis=0), shards)
    moment = momentum_decay * momentum + grad_rows.astype(jnp.float32)

    update = newton_schulz(both, piece_rows)
    return (update[None], moment[None])


def solution(mesh):
    fine = jax.sharding.Mesh(mesh.devices.reshape(4, 4, 8, 2), ("y", "x", "z", "core"))
    replicas, shards = ("y", "x"), ("z", "core")
    placed = (P(replicas, None, shards, None), P(shards, None, replicas, None), P(), P())
    return jax.shard_map(
        body,
        mesh=fine,
        in_specs=placed,
        out_specs=(P(replicas, shards, None), P(shards, None, replicas, None)),
        check_vma=False,
    )
```

```python
import jax
import jax.numpy as jnp
from jax import lax
from jax.experimental import pallas as pl
from jax.experimental.pallas import tpu as pltpu
from jax.sharding import PartitionSpec as P

D = 1536
ITERS = 2
TILE = 512

momentum_decay = 0.95
linear_coef = 3.4445
cubic_coef = -4.775
quintic_coef = 2.0315


def swap(value, axis):
    return lax.all_to_all(value, axis, split_axis=0, concat_axis=0, tiled=True)


def shift(value, axis, by):
    count = lax.axis_size(axis)
    return lax.ppermute(value, axis, [(i, (i + by) % count) for i in range(count)])


def core_swap(value):
    return lax.ppermute(value, "core", [(0, 1), (1, 0)])


def pick_blocks(blocks, order):
    return blocks.at[order].get(mode="promise_in_bounds")


def after(value, other):
    return lax.optimization_barrier((value, other))


def spread_sums(picks, axes):
    places = [lax.axis_index(axis) for axis in axes]
    counts = [lax.axis_size(axis) for axis in axes]
    target = [
        lambda by, pick=pick, place=place, count=count: pick(lax.rem(place + by, count))
        for pick, place, count in zip(picks, places, counts)
    ]
    near = [
        [shift(block(1), axis, 1), shift(block(count - 1), axis, -1)]
        for block, axis, count in zip(target, axes, counts)
    ]
    far = []
    for n, (block, axis) in enumerate(zip(target, axes)):
        sent = block(2)
        if n > 0:
            sent, near[n][0] = after(sent, near[n][0])
        far.append(shift(sent, axis, 2))
    totals = []
    for n, block in enumerate(target):
        total = block(0).astype(jnp.float32)
        for part in near[n] + [far[n]]:
            total = total + part.astype(jnp.float32)
        totals.append(total)
    return totals, near[-1][0]


def ring_gather(piece, axis):
    rows = piece.shape[0]
    forth, back = piece, piece
    pieces = [piece]
    for _ in range(lax.axis_size(axis) // 2 - 1):
        forth, back = shift(forth, axis, 1), shift(back, axis, -1)
        pieces += [forth, back]
    return pieces + [shift(forth[: rows // 2], axis, 1), shift(back[rows // 2 :], axis, -1)]


def newton_schulz_kernel(*refs):
    scratch = 8
    pieces, out_ref = refs[: -scratch - 1], refs[-scratch - 1]
    source, result, gram_ref, poly_ref, kept_ref, diag_ref, square_ref, sems = refs[-scratch:]
    tiles = D // TILE
    small = TILE // 2
    contract_last = (((1,), (1,)), ((), ()))
    copies, start = [], 0
    for n, piece in enumerate(pieces):
        height = piece.shape[0]
        copies.append(pltpu.make_async_copy(piece, source.at[pl.ds(start, height), :], sems.at[n]))
        start += height
    for copy in copies:
        copy.start()
    for copy in copies:
        copy.wait()

    def symmetric(product, finish):
        for t in range(tiles):
            i, j = ((0, 1), (0, 2), (1, 2))[t]
            for row, column, height, diagonal in (
                (i * TILE, j * TILE, TILE, False),
                (i * TILE, j * TILE + small, TILE, False),
                (t * TILE, t * TILE, TILE, True),
                (t * TILE + small, t * TILE + small, small, True),
            ):
                rows, columns = slice(row, row + height), slice(column, column + small)
                finish(rows, columns, diagonal, product(rows, columns))

    def store(target, rows, columns, diagonal, low):
        target[rows, columns] = low
        if not diagonal:
            target[columns, rows] = low.T
        elif rows.stop - rows.start == TILE:
            target[columns, rows.start + small : rows.stop] = low[small:, :].T

    def sweep(turn, carry):
        diag_ref[...] = jnp.zeros_like(diag_ref)
        square_ref[...] = jnp.zeros_like(square_ref)

        def gram_product(rows, columns):
            return lax.dot_general(
                source[rows, :], source[columns, :], contract_last, preferred_element_type=jnp.float32
            )

        def gram_finish(rows, columns, diagonal, total):
            if diagonal:
                down = lax.broadcasted_iota(jnp.int32, total.shape, 0)
                along = lax.broadcasted_iota(jnp.int32, total.shape, 1)
                diag_ref[...] += jnp.sum(jnp.where(down == along, total, 0.0), axis=0, keepdims=True)
            store(gram_ref, rows, columns, diagonal, total.astype(jnp.bfloat16))

        symmetric(gram_product, gram_finish)
        norm = jnp.sqrt(jnp.sum(diag_ref[...])) + 1e-07
        inverse = jnp.where(turn == 0, 1.0 / norm, 1.0)
        cubic = cubic_coef * (inverse * inverse)
        quintic = quintic_coef * (inverse * inverse) * (inverse * inverse)

        def poly_product(rows, columns):
            return jnp.dot(gram_ref[rows, :], gram_ref[:, columns], preferred_element_type=jnp.float32)

        def poly_finish(rows, columns, diagonal, total):
            value = cubic * gram_ref[rows, columns].astype(jnp.float32) + quintic * total
            store(poly_ref, rows, columns, diagonal, value.astype(jnp.bfloat16))

        symmetric(poly_product, poly_finish)
        def mix_tile(t, carry):
            rows = pl.ds(pl.multiple_of(t * TILE, TILE), TILE)
            for c in range(0, D, small):
                columns = slice(c, c + small)
                total = jnp.dot(poly_ref[rows, :], source[:, columns], preferred_element_type=jnp.float32)
                mixed = (linear_coef * source[rows, columns].astype(jnp.float32) + total) * inverse
                result[rows, columns] = mixed.astype(jnp.bfloat16)
                square_ref[...] += jnp.sum(mixed * mixed, axis=0, keepdims=True)
                kept_ref[t, :, columns] = mixed[: kept_ref.shape[1], :]
            return carry

        lax.fori_loop(0, tiles, mix_tile, 0)

        def copy_back(t, carry):
            rows = pl.ds(pl.multiple_of(t * small, small), small)
            source[rows, :] = result[rows, :]
            return carry

        lax.fori_loop(0, D // small, copy_back, 0)
        return carry

    lax.fori_loop(0, ITERS, sweep, 0)
    scale = lax.rsqrt(jnp.sum(square_ref[...]) / (D * D) + 1e-06)
    out_ref[...] = (kept_ref[0] * scale).astype(jnp.bfloat16)


def newton_schulz(pieces, rows):
    return pl.pallas_call(
        newton_schulz_kernel,
        out_shape=jax.ShapeDtypeStruct((rows, D), jnp.bfloat16),
        in_specs=[pl.BlockSpec(memory_space=pl.ANY)] * len(pieces),
        out_specs=pl.BlockSpec(memory_space=pltpu.VMEM),
        scratch_shapes=[
            pltpu.VMEM((D, D), jnp.bfloat16),
            pltpu.VMEM((D, D), jnp.bfloat16),
            pltpu.VMEM((D, D), jnp.bfloat16),
            pltpu.VMEM((D, D), jnp.bfloat16),
            pltpu.VMEM((D // TILE, rows, D), jnp.float32),
            pltpu.VMEM((1, TILE // 2), jnp.float32),
            pltpu.VMEM((1, TILE // 2), jnp.float32),
            pltpu.SemaphoreType.DMA((len(pieces),)),
        ],
        compiler_params=pltpu.CompilerParams(vmem_limit_bytes=40 * 1024 * 1024),
        cost_estimate=pl.CostEstimate(
            flops=2 * ITERS * 7 * D * D * D // 3, bytes_accessed=D * D * 2, transcendentals=0
        ),
        name="newton_schulz",
    )(*pieces)


def body(grad_parts, momentum_owned, owner_table, step_offset):
    replicas, shards = ("y", "x"), ("z", "core")
    mats, piece_rows = grad_parts.shape[1], grad_parts.shape[2]
    sub_rows = momentum_owned.shape[2]
    owner_slot = (owner_table + step_offset[0]) % mats
    slot_ids = jnp.arange(mats, dtype=jnp.int32)
    owner_order = jnp.sum(
        jnp.where(owner_slot[None, :] == slot_ids[:, None], slot_ids[None, :], 0), axis=1
    )
    momentum = momentum_owned[0]

    tall, across = lax.axis_size("y"), lax.axis_size("x")
    parts = grad_parts.reshape(tall, across, piece_rows, D)
    half = piece_rows // 2

    def upper_for(t):
        return lax.dynamic_slice(parts, (0, t, 0, 0), (tall, 1, half, D)).reshape(tall, half, D)

    def lower_for(t):
        return lax.dynamic_slice(parts, (t, 0, half, 0), (1, across, half, D)).reshape(across, half, D)

    (upper, lower), _ = spread_sums([upper_for, lower_for], ["x", "y"])
    (upper, lower), arrived = spread_sums(
        [lambda t: lax.dynamic_index_in_dim(upper, t, 0, False), lambda t: lax.dynamic_index_in_dim(lower, t, 0, False)],
        ["y", "x"],
    )
    summed = lax.optimization_barrier(jnp.concatenate([upper, lower], axis=0))
    grad = summed.astype(jnp.bfloat16)

    by_slot, _ = after(swap(momentum.astype(jnp.bfloat16), shards), arrived)
    own_momentum = swap(pick_blocks(by_slot, owner_slot), replicas).reshape(piece_rows, D)

    grad_float = grad.astype(jnp.float32)
    moment_here = momentum_decay * own_momentum.astype(jnp.float32) + grad_float
    nesterov = (grad_float + momentum_decay * moment_here).astype(jnp.bfloat16)

    pieces = ring_gather(nesterov, "z")
    both = pieces + [core_swap(piece) for piece in pieces]

    grad_blocks = swap(grad.reshape(mats, sub_rows, D), replicas)
    grad_blocks, _ = after(grad_blocks, pieces[-3])
    grad_rows = swap(jnp.take(grad_blocks, owner_order, axis=0), shards)
    moment = momentum_decay * momentum + grad_rows.astype(jnp.float32)

    update = newton_schulz(both, piece_rows)
    return (update[None], moment[None])


def solution(mesh):
    fine = jax.sharding.Mesh(mesh.devices.reshape(4, 4, 8, 2), ("y", "x", "z", "core"))
    replicas, shards = ("y", "x"), ("z", "core")
    placed = (P(replicas, None, shards, None), P(shards, None, replicas, None), P(), P())
    return jax.shard_map(
        body,
        mesh=fine,
        in_specs=placed,
        out_specs=(P(replicas, shards, None), P(shards, None, replicas, None)),
        check_vma=False,
    )
```

```python
import jax
import jax.numpy as jnp
from jax import lax
from jax.experimental import pallas as pl
from jax.experimental.pallas import tpu as pltpu
from jax.sharding import PartitionSpec as P

D = 1536
ITERS = 2
TILE = 512

momentum_decay = 0.95
linear_coef = 3.4445
cubic_coef = -4.775
quintic_coef = 2.0315


def swap(value, axis):
    return lax.all_to_all(value, axis, split_axis=0, concat_axis=0, tiled=True)


def shift(value, axis, by):
    count = lax.axis_size(axis)
    return lax.ppermute(value, axis, [(i, (i + by) % count) for i in range(count)])


def core_swap(value):
    return lax.ppermute(value, "core", [(0, 1), (1, 0)])


def pick_blocks(blocks, order):
    return blocks.at[order].get(mode="promise_in_bounds")


def after(value, other):
    return lax.optimization_barrier((value, other))


def spread_sums(picks, axes):
    places = [lax.axis_index(axis) for axis in axes]
    counts = [lax.axis_size(axis) for axis in axes]
    target = [
        lambda by, pick=pick, place=place, count=count: pick(lax.rem(place + by, count))
        for pick, place, count in zip(picks, places, counts)
    ]
    near = [
        [shift(block(1), axis, 1), shift(block(count - 1), axis, -1)]
        for block, axis, count in zip(target, axes, counts)
    ]
    far = []
    for n, (block, axis) in enumerate(zip(target, axes)):
        sent = block(2)
        if n > 0:
            sent, near[n][0] = after(sent, near[n][0])
        far.append(shift(sent, axis, 2))
    totals = []
    for n, block in enumerate(target):
        total = block(0).astype(jnp.float32)
        for part in near[n] + [far[n]]:
            total = total + part.astype(jnp.float32)
        totals.append(total)
    return totals, near[-1][0]


def ring_gather(piece, axis):
    rows = piece.shape[0]
    forth, back = piece, piece
    pieces = [piece]
    for _ in range(lax.axis_size(axis) // 2 - 1):
        forth, back = shift(forth, axis, 1), shift(back, axis, -1)
        pieces += [forth, back]
    return pieces + [shift(forth[: rows // 2], axis, 1), shift(back[rows // 2 :], axis, -1)]


def newton_schulz_kernel(*refs):
    scratch = 8
    pieces, out_ref = refs[: -scratch - 1], refs[-scratch - 1]
    source, result, gram_ref, poly_ref, kept_ref, diag_ref, square_ref, sems = refs[-scratch:]
    tiles = D // TILE
    small = TILE // 2
    contract_last = (((1,), (1,)), ((), ()))
    copies, start = [], 0
    for n, piece in enumerate(pieces):
        height = piece.shape[0]
        copies.append(pltpu.make_async_copy(piece, source.at[pl.ds(start, height), :], sems.at[n]))
        start += height
    for copy in copies:
        copy.start()
    for copy in copies:
        copy.wait()

    def symmetric(product, finish):
        for t in range(tiles):
            i, j = ((0, 1), (0, 2), (1, 2))[t]
            for row, column, height, diagonal in (
                (i * TILE, j * TILE, TILE, False),
                (i * TILE, j * TILE + small, TILE, False),
                (t * TILE, t * TILE, TILE, True),
                (t * TILE + small, t * TILE + small, small, True),
            ):
                rows, columns = slice(row, row + height), slice(column, column + small)
                finish(rows, columns, diagonal, product(rows, columns))

    def store(target, rows, columns, diagonal, low):
        target[rows, columns] = low
        if not diagonal:
            target[columns, rows] = low.T
        elif rows.stop - rows.start == TILE:
            target[columns, rows.start + small : rows.stop] = low[small:, :].T

    def sweep(turn, carry):
        diag_ref[...] = jnp.zeros_like(diag_ref)
        square_ref[...] = jnp.zeros_like(square_ref)

        def gram_product(rows, columns):
            return lax.dot_general(
                source[rows, :], source[columns, :], contract_last, preferred_element_type=jnp.float32
            )

        def gram_finish(rows, columns, diagonal, total):
            if diagonal:
                down = lax.broadcasted_iota(jnp.int32, total.shape, 0)
                along = lax.broadcasted_iota(jnp.int32, total.shape, 1)
                diag_ref[...] += jnp.sum(jnp.where(down == along, total, 0.0), axis=0, keepdims=True)
            store(gram_ref, rows, columns, diagonal, total.astype(jnp.bfloat16))

        symmetric(gram_product, gram_finish)
        norm = jnp.sqrt(jnp.sum(diag_ref[...])) + 1e-07
        inverse = jnp.where(turn == 0, 1.0 / norm, 1.0)
        cubic = cubic_coef * (inverse * inverse)
        quintic = quintic_coef * (inverse * inverse) * (inverse * inverse)

        def poly_product(rows, columns):
            return jnp.dot(gram_ref[rows, :], gram_ref[:, columns], preferred_element_type=jnp.float32)

        def poly_finish(rows, columns, diagonal, total):
            value = cubic * gram_ref[rows, columns].astype(jnp.float32) + quintic * total
            store(poly_ref, rows, columns, diagonal, value.astype(jnp.bfloat16))

        symmetric(poly_product, poly_finish)
        def mix_tile(t, carry):
            rows = pl.ds(pl.multiple_of(t * TILE, TILE), TILE)
            for c in range(0, D, small):
                columns = slice(c, c + small)
                total = jnp.dot(poly_ref[rows, :], source[:, columns], preferred_element_type=jnp.float32)
                mixed = (linear_coef * source[rows, columns].astype(jnp.float32) + total) * inverse
                result[rows, columns] = mixed.astype(jnp.bfloat16)
                square_ref[...] += jnp.sum(mixed * mixed, axis=0, keepdims=True)
                kept_ref[t, :, columns] = mixed[: kept_ref.shape[1], :]
            return carry

        lax.fori_loop(0, tiles, mix_tile, 0)

        def copy_back(t, carry):
            rows = pl.ds(pl.multiple_of(t * small, small), small)
            source[rows, :] = result[rows, :]
            return carry

        lax.fori_loop(0, jnp.where(turn + 1 < ITERS, D // small, 0), copy_back, 0)
        return carry

    lax.fori_loop(0, ITERS, sweep, 0)
    scale = lax.rsqrt(jnp.sum(square_ref[...]) / (D * D) + 1e-06)
    out_ref[...] = (kept_ref[0] * scale).astype(jnp.bfloat16)


def newton_schulz(pieces, rows):
    return pl.pallas_call(
        newton_schulz_kernel,
        out_shape=jax.ShapeDtypeStruct((rows, D), jnp.bfloat16),
        in_specs=[pl.BlockSpec(memory_space=pl.ANY)] * len(pieces),
        out_specs=pl.BlockSpec(memory_space=pltpu.VMEM),
        scratch_shapes=[
            pltpu.VMEM((D, D), jnp.bfloat16),
            pltpu.VMEM((D, D), jnp.bfloat16),
            pltpu.VMEM((D, D), jnp.bfloat16),
            pltpu.VMEM((D, D), jnp.bfloat16),
            pltpu.VMEM((D // TILE, rows, D), jnp.float32),
            pltpu.VMEM((1, TILE // 2), jnp.float32),
            pltpu.VMEM((1, TILE // 2), jnp.float32),
            pltpu.SemaphoreType.DMA((len(pieces),)),
        ],
        compiler_params=pltpu.CompilerParams(vmem_limit_bytes=40 * 1024 * 1024),
        cost_estimate=pl.CostEstimate(
            flops=2 * ITERS * 7 * D * D * D // 3, bytes_accessed=D * D * 2, transcendentals=0
        ),
        name="newton_schulz",
    )(*pieces)


def body(grad_parts, momentum_owned, owner_table, step_offset):
    replicas, shards = ("y", "x"), ("z", "core")
    mats, piece_rows = grad_parts.shape[1], grad_parts.shape[2]
    sub_rows = momentum_owned.shape[2]
    owner_slot = (owner_table + step_offset[0]) % mats
    slot_ids = jnp.arange(mats, dtype=jnp.int32)
    owner_order = jnp.sum(
        jnp.where(owner_slot[None, :] == slot_ids[:, None], slot_ids[None, :], 0), axis=1
    )
    momentum = momentum_owned[0]

    tall, across = lax.axis_size("y"), lax.axis_size("x")
    parts = grad_parts.reshape(tall, across, piece_rows, D)
    half = piece_rows // 2

    def upper_for(t):
        return lax.dynamic_slice(parts, (0, t, 0, 0), (tall, 1, half, D)).reshape(tall, half, D)

    def lower_for(t):
        return lax.dynamic_slice(parts, (t, 0, half, 0), (1, across, half, D)).reshape(across, half, D)

    (upper, lower), _ = spread_sums([upper_for, lower_for], ["x", "y"])
    (upper, lower), arrived = spread_sums(
        [lambda t: lax.dynamic_index_in_dim(upper, t, 0, False), lambda t: lax.dynamic_index_in_dim(lower, t, 0, False)],
        ["y", "x"],
    )
    summed = lax.optimization_barrier(jnp.concatenate([upper, lower], axis=0))
    grad = summed.astype(jnp.bfloat16)

    by_slot, _ = after(swap(momentum.astype(jnp.bfloat16), shards), arrived)
    own_momentum = swap(pick_blocks(by_slot, owner_slot), replicas).reshape(piece_rows, D)

    grad_float = grad.astype(jnp.float32)
    moment_here = momentum_decay * own_momentum.astype(jnp.float32) + grad_float
    nesterov = (grad_float + momentum_decay * moment_here).astype(jnp.bfloat16)

    pieces = ring_gather(nesterov, "z")
    both = pieces + [core_swap(piece) for piece in pieces]

    grad_blocks = swap(grad.reshape(mats, sub_rows, D), replicas)
    grad_blocks, _ = after(grad_blocks, pieces[-3])
    grad_rows = swap(jnp.take(grad_blocks, owner_order, axis=0), shards)
    moment = momentum_decay * momentum + grad_rows.astype(jnp.float32)

    update = newton_schulz(both, piece_rows)
    return (update[None], moment[None])


def solution(mesh):
    fine = jax.sharding.Mesh(mesh.devices.reshape(4, 4, 8, 2), ("y", "x", "z", "core"))
    replicas, shards = ("y", "x"), ("z", "core")
    placed = (P(replicas, None, shards, None), P(shards, None, replicas, None), P(), P())
    return jax.shard_map(
        body,
        mesh=fine,
        in_specs=placed,
        out_specs=(P(replicas, shards, None), P(shards, None, replicas, None)),
        check_vma=False,
    )
```
